32 devices in a mesh: gx: 4 (over y, core), gy: 2 (over x), gz: 4 (over z).
Axes of the slice: x: 2, y: 2, z: 4, core: 2. Of those that a mesh axis runs over, the one named last changes fastest.
Arguments:
- trial: bfloat16 [8, 4, 16, 64, 128], P('gx', 'gy', 'gz'), may hold values from -6 to 6
- onsite: bfloat16 [8, 4, 16, 128, 128], P('gx', 'gy', 'gz'), as said below
- coupling: bfloat16 [3, 8, 4, 16, 128, 128], P(None, 'gx', 'gy', 'gz'), may hold values from -0.1875 to 0.1875
- bonds: int32 [3, 8, 4, 16], P(None, 'gx', 'gy', 'gz'), may hold values 0 or 1
Outputs:
- filtered: float32 [8, 4, 16, 64, 128], P('gx', 'gy', 'gz')
The draws below stay inside these ranges and needn't reach their ends.
Inputs may be any that keep to these rules, and one draw needn't show every extreme that they name: `onsite`: each on-site block is symmetric in its last two dimensions.
All inputs are finite; a program needn't handle non-finite values. No bound on the sum of `bonds` on one device may be relied on, other than what follows from the above.
Results may differ from the reference program's by a relative error of at most 0.0052.
Values may be sent and summed in bfloat16 or wider, within the bound.
A program may use at most 64 MiB of HBM per device.

```python
import jax
import jax.numpy as jnp
from jax import lax

ORB = 128
VEC = 64
STEPS = 5
NX = 8
NY = 4
NZ = 16


def draw_onsite(key, part):
    sigma = (7.0 * ORB) ** (-0.5)
    raw = jax.random.normal(key, (NX, NY, NZ, ORB, ORB), jnp.float32)
    sym = (raw + jnp.swapaxes(raw, -1, -2)) * (sigma * 0.70710678)
    return sym.astype(jnp.bfloat16)


def plant(entries, key, low, high):
    longest = entries.shape.index(max(entries.shape))
    spots = []
    for shift in (0, 1):
        where = [jax.random.randint(jax.random.fold_in(key, axis), (), 0, length) for axis, length in enumerate(entries.shape)]
        where[longest] = (where[longest] + shift) % entries.shape[longest]
        spots.append(tuple(where))
    return entries.at[spots[0]].set(low).at[spots[1]].set(high)


def block_levels(stream_key, dims, split, least, top_value):
    def one(position, shards_of):
        steps = jax.random.uniform(jax.random.fold_in(jax.random.fold_in(stream_key, 6), position), (shards_of,), jnp.float32, least / len(split), top_value / len(split))
        return jnp.repeat(jnp.exp(steps), dims[position] // shards_of).reshape((-1,) + (1,) * (len(dims) - position - 1))

    level = one(*split[0])
    for cut in split[1:]:
        level = level * one(*cut)
    return level


def normal_values(stream_key, extent, scale, most, split=(), held_as=jnp.bfloat16):
    result = jax.random.normal(stream_key, extent, jnp.float32) * scale
    if len(split) > 0:
        result = block_levels(stream_key, extent, split, -0.22, 0.18) * result
    return jnp.clip(result, min=-most, max=most).astype(held_as)


def setup_inputs(seed: int = 0) -> dict:
    keys = jax.random.split(jax.random.key(seed), 5)
    return {
        "trial": normal_values(keys[0], (NX, NY, NZ, VEC, ORB), 1.0, 6.0, ((0, 4), (1, 2), (2, 4))),
        "onsite": draw_onsite(jax.random.fold_in(keys[4], 71), 0),
        "coupling": normal_values(keys[2], (3, NX, NY, NZ, ORB, ORB), (7 * ORB) ** -0.5, 0.1875, ((1, 4), (2, 2), (3, 4))),
        "bonds": plant((jax.random.randint(keys[3], (3, NX, NY, NZ), 0, 8) < 7).astype(jnp.int32), jax.random.fold_in(keys[3], 1), 0, 1),
    }


center_shift = 0.25
half_inverse = 0.5


def block_apply(blocks, vecs):
    return jnp.einsum("...pq,...kq->...kp", blocks.astype(jnp.float32), vecs.astype(jnp.float32))


def block_transposed(blocks, vecs):
    return jnp.einsum("...pq,...kp->...kq", blocks.astype(jnp.float32), vecs.astype(jnp.float32))


def apply_hamiltonian(vecs, onsite, coupling, masks):
    padded = jnp.pad(vecs, ((1, 1), (1, 1), (1, 1), (0, 0), (0, 0)))

    def one_slice(index):
        here = lax.dynamic_index_in_dim(vecs, index, 0, keepdims=False)
        after = lax.dynamic_index_in_dim(padded, index + 2, 0, keepdims=False)[1:-1, 1:-1]
        before = lax.dynamic_index_in_dim(padded, index, 0, keepdims=False)[1:-1, 1:-1]
        local_site = lax.dynamic_index_in_dim(onsite, index, 0, keepdims=False)
        blocks = lax.dynamic_index_in_dim(coupling, index, 1, keepdims=False)
        mask_here = lax.dynamic_index_in_dim(masks, index, 1, keepdims=False)
        below = jnp.maximum(index - 1, 0).astype(jnp.int32)
        prev_blocks = lax.dynamic_index_in_dim(coupling, below, 1, keepdims=False)
        prev_mask = lax.dynamic_index_in_dim(masks, below, 1, keepdims=False)[0] * (index > 0).astype(jnp.float32)
        total = block_apply(local_site, here)
        total = total + block_apply(blocks[0], after) * mask_here[0][..., None, None]
        total = total + block_transposed(prev_blocks[0], before) * prev_mask[..., None, None]
        upper_y = jnp.concatenate([here[1:], jnp.zeros_like(here[:1])], axis=0)
        total = total + block_apply(blocks[1], upper_y) * mask_here[1][..., None, None]
        term_y = block_transposed(blocks[1], here) * mask_here[1][..., None, None]
        total = total + jnp.concatenate([jnp.zeros_like(term_y[:1]), term_y[:-1]], axis=0)
        upper_z = jnp.concatenate([here[:, 1:], jnp.zeros_like(here[:, :1])], axis=1)
        total = total + block_apply(blocks[2], upper_z) * mask_here[2][..., None, None]
        term_z = block_transposed(blocks[2], here) * mask_here[2][..., None, None]
        total = total + jnp.concatenate([jnp.zeros_like(term_z[:, :1]), term_z[:, :-1]], axis=1)
        return total

    return lax.map(one_slice, jnp.arange(vecs.shape[0], dtype=jnp.int32))


def reference(trial, onsite, coupling, bonds):
    masks = bonds.astype(jnp.float32)

    def scaled(vecs):
        image = apply_hamiltonian(vecs, onsite, coupling, masks)
        return half_inverse * (image - center_shift * vecs.astype(jnp.float32))

    previous = trial
    current = scaled(trial).astype(jnp.bfloat16)
    for step in range(STEPS - 2):
        following = (2.0 * scaled(current) - previous.astype(jnp.float32)).astype(jnp.bfloat16)
        previous = current
        current = following
    return 2.0 * scaled(current) - previous.astype(jnp.float32)
```

```python
import functools

import jax
import jax.numpy as jnp
from jax import lax
from jax.experimental import pallas as pl
from jax.experimental.pallas import tpu as pltpu
from jax.sharding import PartitionSpec as P

STEPS = 5

center_shift = 0.25
half_inverse = 0.5

BF16 = jnp.bfloat16
F32 = jnp.float32
MESH = pl.DeviceIdType.MESH
AXES = ("gx", "gy", "gz")


def apply_block(vec, block):
    return lax.dot_general(vec, block, (((1,), (1,)), ((), ())), preferred_element_type=F32)


def apply_transposed(vec, block):
    return lax.dot_general(vec, block, (((1,), (0,)), ((), ())), preferred_element_type=F32)


def kernel(sizes, bonds, trial, onsite, coupling, out, vecs, blocks, acc,
           above_x, above_y, above_z, below_x, below_y, below_z,
           part_x, part_y, part_z, send_sem, recv_sem):
    nx, ny, nz = trial.shape[:3]
    order = [0, nz - 1] + list(range(1, nz - 1)) if nz > 1 else [0]
    place = {z: i for i, z in enumerate(order)}
    chunks = [(0, min(2, nz))] + ([(2, nz)] if nz > 2 else [])

    me = [lax.axis_index(a) for a in AXES]
    has_up = [me[d] < sizes[d] - 1 for d in range(3)]
    has_down = [me[d] > 0 for d in range(3)]

    def copies(slot, chunk):
        lo, hi = chunks[chunk]
        zs = pl.ds(lo, hi - lo)
        rows = [
            (0, -1, vecs.at[slot, zs, 0], above_x.at[slot, zs]),
            (0, 1, part_x.at[slot, zs], below_x.at[slot, zs]),
            (1, -1, vecs.at[slot, zs, :, 0], above_y.at[slot, zs]),
            (1, 1, part_y.at[slot, zs], below_y.at[slot, zs]),
        ]
        if chunk == 0:
            rows += [
                (2, -1, vecs.at[slot, place[0]], above_z.at[slot]),
                (2, 1, part_z.at[slot], below_z.at[slot]),
            ]
        result = []
        for i, (d, way, src, dst) in enumerate(rows):
            copy = pltpu.make_async_remote_copy(
                src_ref=src, dst_ref=dst,
                send_sem=send_sem.at[slot, chunk, i], recv_sem=recv_sem.at[slot, chunk, i],
                device_id={AXES[d]: me[d] + way}, device_id_type=MESH)
            sends = has_up[d] if way > 0 else has_down[d]
            receives = has_down[d] if way > 0 else has_up[d]
            result.append((d, way, copy, sends, receives))
        return result

    def start(slot, chunk, way):
        for d, w, copy, sends, _ in copies(slot, chunk):
            if w == way:
                pl.when(sends)(copy.start)

    def finish(slot, chunk):
        for d, w, copy, sends, receives in copies(slot, chunk):
            pl.when(sends)(copy.wait_send)
            pl.when(receives)(copy.wait_recv)

    def cells(chunk):
        lo, hi = chunks[chunk]
        return [(i, order[i], x, y) for i in range(lo, hi) for x in range(nx) for y in range(ny)]

    def partials(slot, chunk):
        for i, z, x, y in cells(chunk):
            v = vecs[slot, i, x, y]
            if x == nx - 1:
                part_x[slot, i, y] = apply_transposed(v, blocks[0, x, y, z]).astype(BF16)
            if y == ny - 1:
                part_y[slot, i, x] = apply_transposed(v, blocks[1, x, y, z]).astype(BF16)
            if z == nz - 1:
                part_z[slot, x, y] = apply_transposed(v, blocks[2, x, y, z]).astype(BF16)

    def local_terms(slot):
        for chunk in range(len(chunks)):
            for i, z, x, y in cells(chunk):
                v = vecs[slot, i, x, y]
                total = apply_transposed(v, onsite[x, y, z])
                if x + 1 < nx:
                    total += apply_block(vecs[slot, i, x + 1, y], blocks[0, x, y, z])
                if x > 0:
                    total += apply_transposed(vecs[slot, i, x - 1, y], blocks[0, x - 1, y, z])
                if y + 1 < ny:
                    total += apply_block(vecs[slot, i, x, y + 1], blocks[1, x, y, z])
                if y > 0:
                    total += apply_transposed(vecs[slot, i, x, y - 1], blocks[1, x, y - 1, z])
                if z + 1 < nz:
                    total += apply_block(vecs[slot, place[z + 1], x, y], blocks[2, x, y, z])
                if z > 0:
                    total += apply_transposed(vecs[slot, place[z - 1], x, y], blocks[2, x, y, z - 1])
                acc[i, x, y] = total - center_shift * v.astype(F32)

    def whole(slot, i, z, x, y):
        total = acc[i, x, y]
        if x == nx - 1:
            total += apply_block(above_x[slot, i, y], blocks[0, x, y, z])
        if x == 0:
            total += below_x[slot, i, y].astype(F32)
        if y == ny - 1:
            total += apply_block(above_y[slot, i, x], blocks[1, x, y, z])
        if y == 0:
            total += below_y[slot, i, x].astype(F32)
        if z == nz - 1:
            total += apply_block(above_z[slot, x, y], blocks[2, x, y, z])
        if z == 0:
            total += below_z[slot, x, y].astype(F32)
        return total

    barrier = pltpu.get_barrier_semaphore()
    count = jnp.int32(0)
    for d in range(3):
        for way, there in ((1, has_up[d]), (-1, has_down[d])):
            pl.when(there)(functools.partial(
                pl.semaphore_signal, barrier, inc=1,
                device_id={AXES[d]: me[d] + way}, device_id_type=MESH))
            count += there.astype(jnp.int32)

    for d, (above, below) in enumerate(((above_x, below_x), (above_y, below_y), (above_z, below_z))):
        @pl.when(jnp.logical_not(has_up[d]))
        def _():
            above[...] = jnp.zeros_like(above)

        @pl.when(jnp.logical_not(has_down[d]))
        def _():
            below[...] = jnp.zeros_like(below)

    for i, z in enumerate(order):
        for x in range(nx):
            for y in range(ny):
                vecs[0, i, x, y] = trial[x, y, z]
                vecs[1, i, x, y] = jnp.zeros(trial.shape[3:], BF16)
                for d in range(3):
                    bond = bonds[d, x, y, z].astype(F32)
                    blocks[d, x, y, z] = (coupling[d, x, y, z].astype(F32) * bond).astype(BF16)

    pl.semaphore_wait(barrier, count)
    for chunk in range(len(chunks)):
        start(0, chunk, -1)
        partials(0, chunk)
        start(0, chunk, 1)

    def step(k, carry):
        slot = lax.rem(k, 2)
        other = 1 - slot
        scale = jnp.where(k == 0, half_inverse, 1.0)
        keep = jnp.where(k == 0, 0.0, 1.0)
        local_terms(slot)
        for chunk in range(len(chunks)):
            finish(slot, chunk)
            for i, z, x, y in cells(chunk):
                before = vecs[other, i, x, y].astype(F32)
                vecs[other, i, x, y] = (scale * whole(slot, i, z, x, y) - keep * before).astype(BF16)
            start(other, chunk, -1)
            partials(other, chunk)
            start(other, chunk, 1)
        return carry

    lax.fori_loop(0, STEPS - 1, step, 0)
    slot = (STEPS - 1) % 2
    local_terms(slot)
    for chunk in range(len(chunks)):
        finish(slot, chunk)
        for i, z, x, y in cells(chunk):
            out[x, y, z] = whole(slot, i, z, x, y) - vecs[1 - slot, i, x, y].astype(F32)


def shards(sizes, trial, onsite, coupling, bonds):
    nx, ny, nz, k, q = trial.shape
    vmem = pl.BlockSpec(memory_space=pltpu.VMEM)
    smem = pl.BlockSpec(memory_space=pltpu.SMEM)
    faces = [(2, nz, ny, k, q), (2, nz, nx, k, q), (2, nx, ny, k, q)]
    return pl.pallas_call(
        functools.partial(kernel, sizes),
        out_shape=jax.ShapeDtypeStruct(trial.shape, F32),
        in_specs=[smem, vmem, vmem, vmem],
        out_specs=vmem,
        scratch_shapes=[
            pltpu.VMEM((2, nz, nx, ny, k, q), BF16),
            pltpu.VMEM(coupling.shape, BF16),
            pltpu.VMEM((nz, nx, ny, k, q), F32),
            *[pltpu.VMEM(f, BF16) for f in faces],
            *[pltpu.VMEM(f, BF16) for f in faces],
            *[pltpu.VMEM(f, BF16) for f in faces],
            pltpu.SemaphoreType.DMA((2, 2, 6)),
            pltpu.SemaphoreType.DMA((2, 2, 6)),
        ],
        compiler_params=pltpu.CompilerParams(
            collective_id=0, has_side_effects=True, vmem_limit_bytes=32 * 1024 * 1024),
    )(bonds, trial, onsite, coupling)


def solution(mesh):
    placed = (
        P("gx", "gy", "gz", None, None),
        P("gx", "gy", "gz", None, None),
        P(None, "gx", "gy", "gz", None, None),
        P(None, "gx", "gy", "gz"),
    )
    return jax.shard_map(
        functools.partial(shards, tuple(mesh.shape[a] for a in AXES)),
        mesh=mesh,
        in_specs=placed,
        out_specs=P("gx", "gy", "gz", None, None),
        check_vma=False,
    )
```

```python
import functools

import jax
import jax.numpy as jnp
from jax import lax
from jax.experimental import pallas as pl
from jax.experimental.pallas import tpu as pltpu
from jax.sharding import PartitionSpec as P

STEPS = 5

center_shift = 0.25
half_inverse = 0.5

BF16 = jnp.bfloat16
F32 = jnp.float32
MESH = pl.DeviceIdType.MESH
AXES = ("gx", "gy", "gz")


def product(vec, block):
    return lax.dot_general(vec, block, (((1,), (0,)), ((), ())), preferred_element_type=F32)


def side_by_side(parts):
    return parts[0] if len(parts) == 1 else jnp.concatenate(parts, axis=1)


def kernel(sizes, planes, bonds_in, trial, onsite, coupling, out, bonds, vecs, raw, acc,
           with_y, with_near, with_above, for_parts,
           above_x, above_y, above_z, below_x, below_y, below_z,
           part_x, part_y, part_z, send_sem, recv_sem, load_sem):
    nx, ny, nz, rows, q = trial.shape
    order = [0, nz - 1] + list(range(1, nz - 1)) if nz > 1 else [0]
    place = {z: i for i, z in enumerate(order)}
    chunks = [(lo, min(lo + planes, nz)) for lo in range(0, nz, planes)]
    length = (nx, ny, nz)

    me = [lax.axis_index(a) for a in AXES]
    has_up = [me[d] < sizes[d] - 1 for d in range(3)]
    has_down = [me[d] > 0 for d in range(3)]

    def near(z, x, y):
        here = (x, y, z)
        found = []
        for d in (0, 2):
            for way in (-1, 1):
                there = list(here)
                there[d] += way
                if 0 <= there[d] < length[d]:
                    found.append((d, way, tuple(there)))
        return found

    def tops(z, x, y):
        here = (x, y, z)
        return [d for d in range(3) if here[d] == length[d] - 1]

    def copies(slot, chunk):
        lo, hi = chunks[chunk]
        zs = pl.ds(lo, hi - lo)
        result = []

        def add(i, d, way, src, dst):
            def make():
                return pltpu.make_async_remote_copy(
                    src_ref=src, dst_ref=dst,
                    send_sem=send_sem.at[slot, chunk, i], recv_sem=recv_sem.at[slot, chunk, i],
                    device_id={AXES[d]: me[d] + way}, device_id_type=MESH)
            sends = has_up[d] if way > 0 else has_down[d]
            receives = has_down[d] if way > 0 else has_up[d]
            result.append((i, make, sends, receives))

        add(0, 1, -1, vecs.at[slot, zs, :, 0], above_y.at[slot, zs])
        add(1, 1, 1, part_y.at[slot, zs], below_y.at[slot, zs])
        if lo <= place[0] < hi:
            add(2, 2, -1, vecs.at[slot, place[0]], above_z.at[slot])
        if lo <= place[nz - 1] < hi:
            add(3, 2, 1, part_z.at[slot], below_z.at[slot])
        add(4, 0, -1, vecs.at[slot, zs, 0], above_x.at[slot, zs])
        add(5, 0, 1, part_x.at[slot, zs], below_x.at[slot, zs])
        return result

    def start(slot, chunk, ways):
        for i, make, sends, _ in copies(slot, chunk):
            if i % 2 in ways:
                @pl.when(sends)
                def _():
                    make().start()

    def receive(slot, chunk):
        lo, hi = chunks[chunk]
        for other in range(len(chunks)):
            for i, make, sends, receives in copies(slot, other):
                if (i == 2 and lo <= place[nz - 1] < hi) or (i == 3 and lo <= place[0] < hi) or (
                        i not in (2, 3) and other == chunk):
                    @pl.when(sends)
                    def _():
                        make().wait_send()

                    @pl.when(receives)
                    def _():
                        make().wait_recv()

    def cells(chunk):
        lo, hi = chunks[chunk]
        return [(i, order[i], x, y) for i in range(lo, hi) for x in range(nx) for y in range(ny)]

    def partials(slot, chunk):
        for i, z, x, y in cells(chunk):
            dims = tops(z, x, y)
            if not dims:
                continue
            sums = product(vecs[slot, i, x, y], for_parts[i, x, y, :, pl.ds(0, len(dims) * q)]).astype(BF16)
            for n, d in enumerate(dims):
                part = sums[:, n * q:(n + 1) * q]
                if d == 0:
                    part_x[slot, i, y] = part
                elif d == 1:
                    part_y[slot, i, x] = part
                else:
                    part_z[slot, x, y] = part

    def local_terms(slot):
        for i, z in enumerate(order):
            for x in range(nx):
                line = product(side_by_side([vecs[slot, i, x, y] for y in range(ny)]), with_y[i, x])
                for y in range(ny):
                    total = line[:, y * q:(y + 1) * q]
                    others = near(z, x, y)
                    if others:
                        total += product(
                            side_by_side([vecs[slot, place[c[2]], c[0], c[1]] for _, _, c in others]),
                            with_near[i, x, y, pl.ds(0, len(others) * q)])
                    acc[i, x, y] = total - center_shift * vecs[slot, i, x, y].astype(F32)

    def whole(slot, i, z, x, y):
        total = acc[i, x, y]
        dims = tops(z, x, y)
        if dims:
            given = {0: lambda: above_x[slot, i, y], 1: lambda: above_y[slot, i, x], 2: lambda: above_z[slot, x, y]}
            total += product(side_by_side([given[d]() for d in dims]), with_above[i, x, y, pl.ds(0, len(dims) * q)])
        if x == 0:
            total += below_x[slot, i, y].astype(F32)
        if y == 0:
            total += below_y[slot, i, x].astype(F32)
        if z == 0:
            total += below_z[slot, x, y].astype(F32)
        return total

    def masked(d, i, z, x, y):
        return (raw[i, d, x, y].astype(F32) * bonds[d, x, y, z].astype(F32)).astype(BF16)

    barrier = pltpu.get_barrier_semaphore()
    count = jnp.int32(0)
    for d in range(3):
        for way, there in ((1, has_up[d]), (-1, has_down[d])):
            pl.when(there)(functools.partial(
                pl.semaphore_signal, barrier, inc=1,
                device_id={AXES[d]: me[d] + way}, device_id_type=MESH))
            count += there.astype(jnp.int32)

    loads_vec = [pltpu.make_async_copy(trial.at[:, :, z], vecs.at[0, i], load_sem.at[0, i])
                 for i, z in enumerate(order)]
    load_bonds = pltpu.make_async_copy(bonds_in, bonds, load_sem.at[2, 0])
    loads_block = [pltpu.make_async_copy(coupling.at[:, :, :, z], raw.at[i], load_sem.at[1, i])
                   for i, z in enumerate(order)]
    loads_site = [[pltpu.make_async_copy(
        onsite.at[:, y, z], with_y.at[i, :, pl.ds(y * q, q), pl.ds(y * q, q)], load_sem.at[3 + y, i])
        for y in range(ny)] for i, z in enumerate(order)]
    for copy in loads_vec + [load_bonds] + loads_block + sum(loads_site, []):
        copy.start()

    for d, (above, below) in enumerate(((above_x, below_x), (above_y, below_y), (above_z, below_z))):
        @pl.when(jnp.logical_not(has_up[d]))
        def _():
            above[...] = jnp.zeros_like(above)

        @pl.when(jnp.logical_not(has_down[d]))
        def _():
            below[...] = jnp.zeros_like(below)

    vecs[1] = jnp.zeros(vecs.shape[1:], BF16)
    if ny > 2:
        for i in range(nz):
            for x in range(nx):
                for y in range(ny):
                    for other in range(ny):
                        if abs(other - y) > 1:
                            with_y[i, x, pl.ds(y * q, q), pl.ds(other * q, q)] = jnp.zeros((q, q), BF16)

    pl.semaphore_wait(barrier, count)
    for copy in loads_vec:
        copy.wait()
    for chunk in range(len(chunks)):
        start(0, chunk, (0,))
    load_bonds.wait()
    for chunk in range(len(chunks)):
        for i in range(*chunks[chunk]):
            loads_block[i].wait()
        for i, z, x, y in cells(chunk):
            for n, d in enumerate(tops(z, x, y)):
                for_parts[i, x, y, :, pl.ds(n * q, q)] = masked(d, i, z, x, y)
        partials(0, chunk)
        start(0, chunk, (1,))
    for chunk in range(len(chunks)):
        for i, z, x, y in cells(chunk):
            here = (x, y, z)
            dims = tops(z, x, y)
            for d in range(3):
                if d in dims:
                    n = dims.index(d)
                    with_above[i, x, y, pl.ds(n * q, q)] = for_parts[i, x, y, :, pl.ds(n * q, q)].T
                    continue
                block = masked(d, i, z, x, y)
                if d == 1:
                    with_y[i, x, pl.ds(y * q, q), pl.ds((y + 1) * q, q)] = block
                    with_y[i, x, pl.ds((y + 1) * q, q), pl.ds(y * q, q)] = block.T
                    continue
                there = list(here)
                there[d] += 1
                up = [(e, way) for e, way, _ in near(z, x, y)].index((d, 1))
                down = [(e, way) for e, way, _ in near(there[2], there[0], there[1])].index((d, -1))
                with_near[i, x, y, pl.ds(up * q, q)] = block.T
                with_near[place[there[2]], there[0], there[1], pl.ds(down * q, q)] = block
    for copy in sum(loads_site, []):
        copy.wait()

    def step(k, carry):
        slot = lax.rem(k, 2)
        other = 1 - slot
        scale = jnp.where(k == 0, half_inverse, 1.0)
        keep = jnp.where(k == 0, 0.0, 1.0)
        local_terms(slot)
        for chunk in range(len(chunks)):
            receive(slot, chunk)
            for i, z, x, y in cells(chunk):
                before = vecs[other, i, x, y].astype(F32)
                vecs[other, i, x, y] = (scale * whole(slot, i, z, x, y) - keep * before).astype(BF16)
            start(other, chunk, (0,))
            partials(other, chunk)
            start(other, chunk, (1,))
        return carry

    lax.fori_loop(0, STEPS - 1, step, 0)
    slot = (STEPS - 1) % 2
    local_terms(slot)
    for chunk in range(len(chunks)):
        receive(slot, chunk)
        for i, z, x, y in cells(chunk):
            out[x, y, z] = whole(slot, i, z, x, y) - vecs[1 - slot, i, x, y].astype(F32)


def shards(sizes, trial, onsite, coupling, bonds):
    nx, ny, nz, k, q = trial.shape
    planes = 1
    hbm = pl.BlockSpec(memory_space=pltpu.HBM)
    faces = [(2, nz, ny, k, q), (2, nz, nx, k, q), (2, nx, ny, k, q)]
    return pl.pallas_call(
        functools.partial(kernel, sizes, planes),
        out_shape=jax.ShapeDtypeStruct(trial.shape, F32),
        in_specs=[hbm, hbm, hbm, hbm],
        out_specs=pl.BlockSpec(memory_space=pltpu.VMEM),
        scratch_shapes=[
            pltpu.SMEM(bonds.shape, jnp.int32),
            pltpu.VMEM((2, nz, nx, ny, k, q), BF16),
            pltpu.VMEM((nz, 3, nx, ny, q, q), BF16),
            pltpu.VMEM((nz, nx, ny, k, q), F32),
            pltpu.VMEM((nz, nx, ny * q, ny * q), BF16),
            pltpu.VMEM((nz, nx, ny, 4 * q, q), BF16),
            pltpu.VMEM((nz, nx, ny, 3 * q, q), BF16),
            pltpu.VMEM((nz, nx, ny, q, 3 * q), BF16),
            *[pltpu.VMEM(f, BF16) for f in faces],
            *[pltpu.VMEM(f, BF16) for f in faces],
            *[pltpu.VMEM(f, BF16) for f in faces],
            pltpu.SemaphoreType.DMA((2, nz, 6)),
            pltpu.SemaphoreType.DMA((2, nz, 6)),
            pltpu.SemaphoreType.DMA((3 + ny, nz)),
        ],
        compiler_params=pltpu.CompilerParams(
            collective_id=0, has_side_effects=True, vmem_limit_bytes=48 * 1024 * 1024),
    )(bonds, trial, onsite, coupling)


def solution(mesh):
    placed = (
        P("gx", "gy", "gz", None, None),
        P("gx", "gy", "gz", None, None),
        P(None, "gx", "gy", "gz", None, None),
        P(None, "gx", "gy", "gz"),
    )
    return jax.shard_map(
        functools.partial(shards, tuple(mesh.shape[a] for a in AXES)),
        mesh=mesh,
        in_specs=placed,
        out_specs=P("gx", "gy", "gz", None, None),
        check_vma=False,
    )
```

```python
import functools

import jax
import jax.numpy as jnp
from jax import lax
from jax.experimental import pallas as pl
from jax.experimental.pallas import tpu as pltpu
from jax.sharding import PartitionSpec as P

STEPS = 5

center_shift = 0.25
half_inverse = 0.5

BF16 = jnp.bfloat16
F32 = jnp.float32
MESH = pl.DeviceIdType.MESH
AXES = ("gx", "gy", "gz")


def product(vec, block):
    return lax.dot_general(vec, block, (((1,), (0,)), ((), ())), preferred_element_type=F32)


def side_by_side(parts):
    return parts[0] if len(parts) == 1 else jnp.concatenate(parts, axis=1)


def kernel(sizes, bonds_in, trial, onsite, coupling, out, bonds, vecs, raw, acc,
           with_y, with_near, with_above, for_parts,
           above_x, above_y, above_z, below_x, below_y, below_z,
           part_x, part_y, part_z, send_sem, recv_sem, load_sem):
    nx, ny, nz, rows, q = trial.shape
    order = [0, nz - 1] + list(range(1, nz - 1)) if nz > 1 else [0]
    place = {z: i for i, z in enumerate(order)}
    chunks = [(i, i + 1) for i in range(nz)]
    length = (nx, ny, nz)

    me = [lax.axis_index(a) for a in AXES]
    has_up = [me[d] < sizes[d] - 1 for d in range(3)]
    has_down = [me[d] > 0 for d in range(3)]

    def near(z, x, y):
        here = (x, y, z)
        found = []
        for d in (0, 2):
            for way in (-1, 1):
                there = list(here)
                there[d] += way
                if 0 <= there[d] < length[d]:
                    found.append((d, way, tuple(there)))
        return found

    def tops(z, x, y):
        here = (x, y, z)
        return [d for d in range(3) if here[d] == length[d] - 1]

    def copies(slot, chunk, first=False):
        i = chunk
        z = order[i]
        result = []

        def add(kind, d, way, src, dst):
            def make():
                return pltpu.make_async_remote_copy(
                    src_ref=src, dst_ref=dst,
                    send_sem=send_sem.at[slot, chunk, kind], recv_sem=recv_sem.at[slot, chunk, kind],
                    device_id={AXES[d]: me[d] + way}, device_id_type=MESH)
            sends = has_up[d] if way > 0 else has_down[d]
            receives = has_down[d] if way > 0 else has_up[d]
            result.append((kind, make, sends, receives))

        add(0, 1, -1, trial.at[:, 0, z] if first else vecs.at[slot, i, :, 0], above_y.at[slot, i])
        add(1, 1, 1, part_y.at[slot, i], below_y.at[slot, i])
        if z == 0:
            add(2, 2, -1, trial.at[:, :, z] if first else vecs.at[slot, i], above_z.at[slot])
        if z == nz - 1:
            add(3, 2, 1, part_z.at[slot], below_z.at[slot])
        add(4, 0, -1, trial.at[0, :, z] if first else vecs.at[slot, i, 0], above_x.at[slot, i])
        add(5, 0, 1, part_x.at[slot, i], below_x.at[slot, i])
        return result

    def start(slot, chunk, ways, first=False):
        for i, make, sends, _ in copies(slot, chunk, first):
            if i % 2 in ways:
                @pl.when(sends)
                def _():
                    make().start()

    def receive(slot, chunk):
        lo, hi = chunks[chunk]
        for other in range(len(chunks)):
            for i, make, sends, receives in copies(slot, other):
                if (i == 2 and lo <= place[nz - 1] < hi) or (i == 3 and lo <= place[0] < hi) or (
                        i not in (2, 3) and other == chunk):
                    @pl.when(sends)
                    def _():
                        make().wait_send()

                    @pl.when(receives)
                    def _():
                        make().wait_recv()

    def cells(chunk):
        lo, hi = chunks[chunk]
        return [(i, order[i], x, y) for i in range(lo, hi) for x in range(nx) for y in range(ny)]

    def partials(slot, chunk):
        for i, z, x, y in cells(chunk):
            dims = tops(z, x, y)
            if not dims:
                continue
            sums = product(vecs[slot, i, x, y], for_parts[i, x, y, :, pl.ds(0, len(dims) * q)]).astype(BF16)
            for n, d in enumerate(dims):
                part = sums[:, n * q:(n + 1) * q]
                if d == 0:
                    part_x[slot, i, y] = part
                elif d == 1:
                    part_y[slot, i, x] = part
                else:
                    part_z[slot, x, y] = part

    def local_terms(slot):
        for i, z in enumerate(order):
            for x in range(nx):
                line = product(side_by_side([vecs[slot, i, x, y] for y in range(ny)]), with_y[i, x])
                for y in range(ny):
                    total = line[:, y * q:(y + 1) * q]
                    others = near(z, x, y)
                    if others:
                        total += product(
                            side_by_side([vecs[slot, place[c[2]], c[0], c[1]] for _, _, c in others]),
                            with_near[i, x, y, pl.ds(0, len(others) * q)])
                    acc[i, x, y] = total - center_shift * vecs[slot, i, x, y].astype(F32)

    def whole(slot, i, z, x, y):
        total = acc[i, x, y]
        dims = tops(z, x, y)
        if dims:
            given = {0: lambda: above_x[slot, i, y], 1: lambda: above_y[slot, i, x], 2: lambda: above_z[slot, x, y]}
            total += product(side_by_side([given[d]() for d in dims]), with_above[i, x, y, pl.ds(0, len(dims) * q)])
        if x == 0:
            total += below_x[slot, i, y].astype(F32)
        if y == 0:
            total += below_y[slot, i, x].astype(F32)
        if z == 0:
            total += below_z[slot, x, y].astype(F32)
        return total

    def masked(d, i, z, x, y):
        return (raw[i, d, x, y].astype(F32) * bonds[d, x, y, z].astype(F32)).astype(BF16)

    barrier = pltpu.get_barrier_semaphore()
    count = jnp.int32(0)
    for d in range(3):
        for way, there in ((1, has_up[d]), (-1, has_down[d])):
            pl.when(there)(functools.partial(
                pl.semaphore_signal, barrier, inc=1,
                device_id={AXES[d]: me[d] + way}, device_id_type=MESH))
            count += there.astype(jnp.int32)

    loads_vec = [pltpu.make_async_copy(trial.at[:, :, z], vecs.at[0, i], load_sem.at[0, i])
                 for i, z in enumerate(order)]
    stores = [pltpu.make_async_copy(acc.at[i], out.at[:, :, z], load_sem.at[0, i]) for i, z in enumerate(order)]
    load_bonds = pltpu.make_async_copy(bonds_in, bonds, load_sem.at[2, 0])
    loads_block = [pltpu.make_async_copy(coupling.at[:, :, :, z], raw.at[i], load_sem.at[1, i])
                   for i, z in enumerate(order)]
    loads_site = [[pltpu.make_async_copy(
        onsite.at[:, y, z], with_y.at[i, :, pl.ds(y * q, q), pl.ds(y * q, q)], load_sem.at[3 + y, i])
        for y in range(ny)] for i, z in enumerate(order)]
    for copy in [load_bonds] + loads_vec + loads_block + sum(loads_site, []):
        copy.start()

    for d, (above, below) in enumerate(((above_x, below_x), (above_y, below_y), (above_z, below_z))):
        @pl.when(jnp.logical_not(has_up[d]))
        def _():
            above[...] = jnp.zeros_like(above)

        @pl.when(jnp.logical_not(has_down[d]))
        def _():
            below[...] = jnp.zeros_like(below)

    vecs[1] = jnp.zeros(vecs.shape[1:], BF16)
    if ny > 2:
        for i in range(nz):
            for x in range(nx):
                for y in range(ny):
                    for other in range(ny):
                        if abs(other - y) > 1:
                            with_y[i, x, pl.ds(y * q, q), pl.ds(other * q, q)] = jnp.zeros((q, q), BF16)

    pl.semaphore_wait(barrier, count)
    for chunk in range(len(chunks)):
        start(0, chunk, (0,), first=True)
    for copy in loads_vec:
        copy.wait()
    load_bonds.wait()
    for chunk in range(len(chunks)):
        for i in range(*chunks[chunk]):
            loads_block[i].wait()
        for i, z, x, y in cells(chunk):
            for n, d in enumerate(tops(z, x, y)):
                for_parts[i, x, y, :, pl.ds(n * q, q)] = masked(d, i, z, x, y)
        partials(0, chunk)
        start(0, chunk, (1,))
    for chunk in range(len(chunks)):
        for i, z, x, y in cells(chunk):
            here = (x, y, z)
            dims = tops(z, x, y)
            for d in range(3):
                if d in dims:
                    n = dims.index(d)
                    with_above[i, x, y, pl.ds(n * q, q)] = for_parts[i, x, y, :, pl.ds(n * q, q)].T
                    continue
                block = masked(d, i, z, x, y)
                if d == 1:
                    with_y[i, x, pl.ds(y * q, q), pl.ds((y + 1) * q, q)] = block
                    with_y[i, x, pl.ds((y + 1) * q, q), pl.ds(y * q, q)] = block.T
                    continue
                there = list(here)
                there[d] += 1
                up = [(e, way) for e, way, _ in near(z, x, y)].index((d, 1))
                down = [(e, way) for e, way, _ in near(there[2], there[0], there[1])].index((d, -1))
                with_near[i, x, y, pl.ds(up * q, q)] = block.T
                with_near[place[there[2]], there[0], there[1], pl.ds(down * q, q)] = block
    for copy in sum(loads_site, []):
        copy.wait()

    def step(k, carry):
        slot = lax.rem(k, 2)
        other = 1 - slot
        scale = jnp.where(k == 0, half_inverse, 1.0)
        keep = jnp.where(k == 0, 0.0, 1.0)
        local_terms(slot)
        for chunk in range(len(chunks)):
            receive(slot, chunk)
            for i, z, x, y in cells(chunk):
                before = vecs[other, i, x, y].astype(F32)
                vecs[other, i, x, y] = (scale * whole(slot, i, z, x, y) - keep * before).astype(BF16)
            start(other, chunk, (0,))
            partials(other, chunk)
            start(other, chunk, (1,))
        return carry

    lax.fori_loop(0, STEPS - 1, step, 0)
    slot = (STEPS - 1) % 2
    local_terms(slot)
    for chunk in range(len(chunks)):
        receive(slot, chunk)
        for i, z, x, y in cells(chunk):
            acc[i, x, y] = whole(slot, i, z, x, y) - vecs[1 - slot, i, x, y].astype(F32)
        for i in range(*chunks[chunk]):
            stores[i].start()
    for copy in stores:
        copy.wait()


def shards(sizes, trial, onsite, coupling, bonds):
    nx, ny, nz, k, q = trial.shape
    hbm = pl.BlockSpec(memory_space=pltpu.HBM)
    faces = [(2, nz, ny, k, q), (2, nz, nx, k, q), (2, nx, ny, k, q)]
    return pl.pallas_call(
        functools.partial(kernel, sizes),
        out_shape=jax.ShapeDtypeStruct(trial.shape, F32),
        in_specs=[hbm, hbm, hbm, hbm],
        out_specs=hbm,
        scratch_shapes=[
            pltpu.SMEM(bonds.shape, jnp.int32),
            pltpu.VMEM((2, nz, nx, ny, k, q), BF16),
            pltpu.VMEM((nz, 3, nx, ny, q, q), BF16),
            pltpu.VMEM((nz, nx, ny, k, q), F32),
            pltpu.VMEM((nz, nx, ny * q, ny * q), BF16),
            pltpu.VMEM((nz, nx, ny, 4 * q, q), BF16),
            pltpu.VMEM((nz, nx, ny, 3 * q, q), BF16),
            pltpu.VMEM((nz, nx, ny, q, 3 * q), BF16),
            *[pltpu.VMEM(f, BF16) for f in faces],
            *[pltpu.VMEM(f, BF16) for f in faces],
            *[pltpu.VMEM(f, BF16) for f in faces],
            pltpu.SemaphoreType.DMA((2, nz, 6)),
            pltpu.SemaphoreType.DMA((2, nz, 6)),
            pltpu.SemaphoreType.DMA((3 + ny, nz)),
        ],
        compiler_params=pltpu.CompilerParams(
            collective_id=0, has_side_effects=True, vmem_limit_bytes=60 * 1024 * 1024),
    )(bonds, trial, onsite, coupling)


def solution(mesh):
    placed = (
        P("gx", "gy", "gz", None, None),
        P("gx", "gy", "gz", None, None),
        P(None, "gx", "gy", "gz", None, None),
        P(None, "gx", "gy", "gz"),
    )
    return jax.shard_map(
        functools.partial(shards, tuple(mesh.shape[a] for a in AXES)),
        mesh=mesh,
        in_specs=placed,
        out_specs=P("gx", "gy", "gz", None, None),
        check_vma=False,
    )
```

```python
import functools

import jax
import jax.numpy as jnp
from jax import lax
from jax.experimental import pallas as pl
from jax.experimental.pallas import tpu as pltpu
from jax.sharding import PartitionSpec as P

STEPS = 5

center_shift = 0.25
half_inverse = 0.5

BF16 = jnp.bfloat16
F32 = jnp.float32
MESH = pl.DeviceIdType.MESH
AXES = ("gx", "gy", "gz")


def product(vec, block):
    return lax.dot_general(vec, block, (((1,), (0,)), ((), ())), preferred_element_type=F32)


def side_by_side(parts):
    return parts[0] if len(parts) == 1 else jnp.concatenate(parts, axis=1)


def kernel(sizes, bonds_in, trial, onsite, coupling, out, bonds, vecs, raw, acc,
           with_y, with_near, with_above, for_parts,
           above_x, above_y, above_z, below_x, below_y, below_z,
           part_x, part_y, part_z, send_sem, recv_sem, load_sem):
    nx, ny, nz, rows, q = trial.shape
    order = [0, nz - 1] + list(range(1, nz - 1)) if nz > 1 else [0]
    place = {z: i for i, z in enumerate(order)}
    chunks = [(i, x) for i in range(nz) for x in range(nx)]
    length = (nx, ny, nz)

    me = [lax.axis_index(a) for a in AXES]
    has_up = [me[d] < sizes[d] - 1 for d in range(3)]
    has_down = [me[d] > 0 for d in range(3)]

    def near(z, x, y):
        here = (x, y, z)
        found = []
        for d in (0, 2):
            for way in (-1, 1):
                there = list(here)
                there[d] += way
                if 0 <= there[d] < length[d]:
                    found.append((d, way, tuple(there)))
        return found

    def tops(z, x, y):
        here = (x, y, z)
        return [d for d in range(3) if here[d] == length[d] - 1]

    def copies(slot, chunk, first=False):
        i, x = chunks[chunk]
        z = order[i]
        result = []

        def add(kind, d, way, src, dst):
            def make():
                return pltpu.make_async_remote_copy(
                    src_ref=src, dst_ref=dst,
                    send_sem=send_sem.at[slot, chunk, kind], recv_sem=recv_sem.at[slot, chunk, kind],
                    device_id={AXES[d]: me[d] + way}, device_id_type=MESH)
            sends = has_up[d] if way > 0 else has_down[d]
            receives = has_down[d] if way > 0 else has_up[d]
            result.append((kind, make, sends, receives))

        add(0, 1, -1, trial.at[x, 0, z] if first else vecs.at[slot, i, x, 0], above_y.at[slot, i, x])
        add(1, 1, 1, part_y.at[slot, i, x], below_y.at[slot, i, x])
        if z == 0:
            add(2, 2, -1, trial.at[x, :, z] if first else vecs.at[slot, i, x], above_z.at[slot, x])
        if z == nz - 1:
            add(3, 2, 1, part_z.at[slot, x], below_z.at[slot, x])
        if x == 0:
            add(4, 0, -1, trial.at[0, :, z] if first else vecs.at[slot, i, 0], above_x.at[slot, i])
        if x == nx - 1:
            add(5, 0, 1, part_x.at[slot, i], below_x.at[slot, i])
        return result

    def start(slot, chunk, ways, first=False):
        for i, make, sends, _ in copies(slot, chunk, first):
            if i % 2 in ways:
                @pl.when(sends)
                def _():
                    make().start()

    def receive(slot, chunk):
        i, x = chunks[chunk]
        last = nz - 1
        for other, (j, w) in enumerate(chunks):
            for kind, make, sends, receives in copies(slot, other):
                needed = {
                    0: other == chunk,
                    1: other == chunk,
                    2: w == x and order[i] == last,
                    3: w == x and order[i] == 0,
                    4: j == i and x == nx - 1,
                    5: j == i and x == 0,
                }[kind]
                if needed:
                    @pl.when(sends)
                    def _():
                        make().wait_send()

                    @pl.when(receives)
                    def _():
                        make().wait_recv()

    def cells(chunk):
        i, x = chunks[chunk]
        return [(i, order[i], x, y) for y in range(ny)]

    def partials(slot, chunk):
        for i, z, x, y in cells(chunk):
            dims = tops(z, x, y)
            if not dims:
                continue
            sums = product(vecs[slot, i, x, y], for_parts[i, x, y, :, pl.ds(0, len(dims) * q)]).astype(BF16)
            for n, d in enumerate(dims):
                part = sums[:, n * q:(n + 1) * q]
                if d == 0:
                    part_x[slot, i, y] = part
                elif d == 1:
                    part_y[slot, i, x] = part
                else:
                    part_z[slot, x, y] = part

    def local_terms(slot):
        for i, z in enumerate(order):
            for x in range(nx):
                line = product(side_by_side([vecs[slot, i, x, y] for y in range(ny)]), with_y[i, x])
                for y in range(ny):
                    total = line[:, y * q:(y + 1) * q]
                    others = near(z, x, y)
                    if others:
                        total += product(
                            side_by_side([vecs[slot, place[c[2]], c[0], c[1]] for _, _, c in others]),
                            with_near[i, x, y, pl.ds(0, len(others) * q)])
                    acc[i, x, y] = total - center_shift * vecs[slot, i, x, y].astype(F32)

    def whole(slot, i, z, x, y):
        total = acc[i, x, y]
        dims = tops(z, x, y)
        if dims:
            given = {0: lambda: above_x[slot, i, y], 1: lambda: above_y[slot, i, x], 2: lambda: above_z[slot, x, y]}
            total += product(side_by_side([given[d]() for d in dims]), with_above[i, x, y, pl.ds(0, len(dims) * q)])
        if x == 0:
            total += below_x[slot, i, y].astype(F32)
        if y == 0:
            total += below_y[slot, i, x].astype(F32)
        if z == 0:
            total += below_z[slot, x, y].astype(F32)
        return total

    def masked(d, i, z, x, y):
        return (raw[i, d, x, y].astype(F32) * bonds[d, x, y, z].astype(F32)).astype(BF16)

    barrier = pltpu.get_barrier_semaphore()
    count = jnp.int32(0)
    for d in range(3):
        for way, there in ((1, has_up[d]), (-1, has_down[d])):
            pl.when(there)(functools.partial(
                pl.semaphore_signal, barrier, inc=1,
                device_id={AXES[d]: me[d] + way}, device_id_type=MESH))
            count += there.astype(jnp.int32)

    loads_vec = [pltpu.make_async_copy(trial.at[:, :, z], vecs.at[0, i], load_sem.at[0, i])
                 for i, z in enumerate(order)]
    stores = [pltpu.make_async_copy(acc.at[i], out.at[:, :, z], load_sem.at[0, i]) for i, z in enumerate(order)]
    load_bonds = pltpu.make_async_copy(bonds_in, bonds, load_sem.at[2, 0])
    loads_block = [pltpu.make_async_copy(coupling.at[:, :, :, z], raw.at[i], load_sem.at[1, i])
                   for i, z in enumerate(order)]
    loads_site = [[pltpu.make_async_copy(
        onsite.at[:, y, z], with_y.at[i, :, pl.ds(y * q, q), pl.ds(y * q, q)], load_sem.at[3 + y, i])
        for y in range(ny)] for i, z in enumerate(order)]
    for copy in [load_bonds] + loads_vec + loads_block + sum(loads_site, []):
        copy.start()

    for d, (above, below) in enumerate(((above_x, below_x), (above_y, below_y), (above_z, below_z))):
        @pl.when(jnp.logical_not(has_up[d]))
        def _():
            above[...] = jnp.zeros_like(above)

        @pl.when(jnp.logical_not(has_down[d]))
        def _():
            below[...] = jnp.zeros_like(below)

    vecs[1] = jnp.zeros(vecs.shape[1:], BF16)
    if ny > 2:
        for i in range(nz):
            for x in range(nx):
                for y in range(ny):
                    for other in range(ny):
                        if abs(other - y) > 1:
                            with_y[i, x, pl.ds(y * q, q), pl.ds(other * q, q)] = jnp.zeros((q, q), BF16)

    pl.semaphore_wait(barrier, count)
    for chunk in range(len(chunks)):
        start(0, chunk, (0,), first=True)
    for copy in loads_vec:
        copy.wait()
    load_bonds.wait()
    for chunk in range(len(chunks)):
        if chunks[chunk][1] == 0:
            loads_block[chunks[chunk][0]].wait()
        for i, z, x, y in cells(chunk):
            for n, d in enumerate(tops(z, x, y)):
                for_parts[i, x, y, :, pl.ds(n * q, q)] = masked(d, i, z, x, y)
        partials(0, chunk)
        start(0, chunk, (1,))
    for chunk in range(len(chunks)):
        for i, z, x, y in cells(chunk):
            here = (x, y, z)
            dims = tops(z, x, y)
            for d in range(3):
                if d in dims:
                    n = dims.index(d)
                    with_above[i, x, y, pl.ds(n * q, q)] = for_parts[i, x, y, :, pl.ds(n * q, q)].T
                    continue
                block = masked(d, i, z, x, y)
                if d == 1:
                    with_y[i, x, pl.ds(y * q, q), pl.ds((y + 1) * q, q)] = block
                    with_y[i, x, pl.ds((y + 1) * q, q), pl.ds(y * q, q)] = block.T
                    continue
                there = list(here)
                there[d] += 1
                up = [(e, way) for e, way, _ in near(z, x, y)].index((d, 1))
                down = [(e, way) for e, way, _ in near(there[2], there[0], there[1])].index((d, -1))
                with_near[i, x, y, pl.ds(up * q, q)] = block.T
                with_near[place[there[2]], there[0], there[1], pl.ds(down * q, q)] = block
    for copy in sum(loads_site, []):
        copy.wait()

    def step(k, carry):
        slot = lax.rem(k, 2)
        other = 1 - slot
        scale = jnp.where(k == 0, half_inverse, 1.0)
        keep = jnp.where(k == 0, 0.0, 1.0)
        local_terms(slot)
        for chunk in range(len(chunks)):
            receive(slot, chunk)
            for i, z, x, y in cells(chunk):
                before = vecs[other, i, x, y].astype(F32)
                vecs[other, i, x, y] = (scale * whole(slot, i, z, x, y) - keep * before).astype(BF16)
            start(other, chunk, (0,))
            partials(other, chunk)
            start(other, chunk, (1,))
        return carry

    lax.fori_loop(0, STEPS - 1, step, 0)
    slot = (STEPS - 1) % 2
    local_terms(slot)
    for chunk in range(len(chunks)):
        receive(slot, chunk)
        for i, z, x, y in cells(chunk):
            acc[i, x, y] = whole(slot, i, z, x, y) - vecs[1 - slot, i, x, y].astype(F32)
        if chunks[chunk][1] == nx - 1:
            stores[chunks[chunk][0]].start()
    for copy in stores:
        copy.wait()


def shards(sizes, trial, onsite, coupling, bonds):
    nx, ny, nz, k, q = trial.shape
    hbm = pl.BlockSpec(memory_space=pltpu.HBM)
    faces = [(2, nz, ny, k, q), (2, nz, nx, k, q), (2, nx, ny, k, q)]
    return pl.pallas_call(
        functools.partial(kernel, sizes),
        out_shape=jax.ShapeDtypeStruct(trial.shape, F32),
        in_specs=[hbm, hbm, hbm, hbm],
        out_specs=hbm,
        scratch_shapes=[
            pltpu.SMEM(bonds.shape, jnp.int32),
            pltpu.VMEM((2, nz, nx, ny, k, q), BF16),
            pltpu.VMEM((nz, 3, nx, ny, q, q), BF16),
            pltpu.VMEM((nz, nx, ny, k, q), F32),
            pltpu.VMEM((nz, nx, ny * q, ny * q), BF16),
            pltpu.VMEM((nz, nx, ny, 4 * q, q), BF16),
            pltpu.VMEM((nz, nx, ny, 3 * q, q), BF16),
            pltpu.VMEM((nz, nx, ny, q, 3 * q), BF16),
            *[pltpu.VMEM(f, BF16) for f in faces],
            *[pltpu.VMEM(f, BF16) for f in faces],
            *[pltpu.VMEM(f, BF16) for f in faces],
            pltpu.SemaphoreType.DMA((2, nz * nx, 6)),
            pltpu.SemaphoreType.DMA((2, nz * nx, 6)),
            pltpu.SemaphoreType.DMA((3 + ny, nz)),
        ],
        compiler_params=pltpu.CompilerParams(
            collective_id=0, has_side_effects=True, vmem_limit_bytes=60 * 1024 * 1024),
    )(bonds, trial, onsite, coupling)


def solution(mesh):
    placed = (
        P("gx", "gy", "gz", None, None),
        P("gx", "gy", "gz", None, None),
        P(None, "gx", "gy", "gz", None, None),
        P(None, "gx", "gy", "gz"),
    )
    return jax.shard_map(
        functools.partial(shards, tuple(mesh.shape[a] for a in AXES)),
        mesh=mesh,
        in_specs=placed,
        out_specs=P("gx", "gy", "gz", None, None),
        check_vma=False,
    )
```
